32 devices in a mesh: wall: 8 (over z, x), span: 4 (over y, core).
Axes of the slice: x: 2, y: 2, z: 4, core: 2. Of those that a mesh axis runs over, the one named last changes fastest.
Arguments:
- velocity: bfloat16 [2, 8, 1536, 4096], P(None, None, 'wall', 'span')
- kx_index: int32 [8], replicated, may hold values from 0 to 5119
- kz_index: int32 [4096], P('span'), may hold values from 0 to 4095
- helm_even: bfloat16 [768, 768], replicated, may hold values from -0.21875 to 0.21875
- helm_odd: bfloat16 [768, 768], replicated, may hold values from -0.21875 to 0.21875
- deriv_even: bfloat16 [768, 768], replicated, may hold values from -0.21875 to 0.21875
- deriv_odd: bfloat16 [768, 768], replicated, may hold values from -0.21875 to 0.21875
Outputs:
- updated: bfloat16 [2, 8, 1536, 4096], P(None, None, 'wall', 'span')
- shear: bfloat16 [2, 8, 1536, 4096], P(None, None, 'wall', 'span')
The draws below stay inside these ranges and needn't reach their ends.
All inputs are finite; a program needn't handle non-finite values.
Results may differ from the reference program's by a relative error of at most 0.008.
Values may be sent and summed in bfloat16 or wider, within the bound.
No kernel may reach another device: no remote copies, remote signals or barrier semaphores. Data moves between devices by JAX's collectives and lax.ppermute only.
A program may use at most 128 MiB of HBM per device.

```python
import jax
import jax.numpy as jnp
from jax import lax

NY = 1536
KZ = 4096
XMODES = 5120
KX = 8


def draw_velocity(key, part):
    key_base, key_plane, key_span = jax.random.split(key, 3)
    plane_ramp = jnp.exp(jnp.log(0.4) + jnp.log(4.0) * jnp.arange(NY, dtype=jnp.float32) / NY)
    plane_ramp = plane_ramp * jnp.exp(jax.random.uniform(key_plane, (NY,), jnp.float32, -0.35, 0.35))
    span_ramp = 0.6 + 0.9 * jnp.arange(KZ, dtype=jnp.float32) / KZ
    span_ramp = span_ramp * jnp.exp(jax.random.uniform(key_span, (KZ,), jnp.float32, -0.35, 0.35))
    base = jax.random.normal(key_base, (2, KX, NY, KZ), jnp.float32)
    return (base * plane_ramp[None, None, :, None] * span_ramp[None, None, None, :]).astype(jnp.bfloat16)


def set_ends(array, rng, smallest, high):
    place = [jax.random.randint(jax.random.fold_in(rng, axis), (), 0, length) for axis, length in enumerate(array.shape)]
    widest = array.shape.index(max(array.shape))
    beside = place[:widest] + [(place[widest] + 1) % array.shape[widest]] + place[widest + 1:]
    return array.at[tuple(place)].set(smallest).at[tuple(beside)].set(high)


def normal_values(own_key, dims, scale, limit, kind=jnp.bfloat16):
    drawn = scale * jax.random.normal(own_key, dims, jnp.float32)
    return jnp.clip(drawn, min=-limit, max=limit).astype(kind)


def setup_inputs(seed: int = 0) -> dict:
    keys = jax.random.split(jax.random.key(seed), 8)
    velocity = draw_velocity(jax.random.fold_in(keys[7], 71), 0)
    kx_index = set_ends(jax.random.randint(keys[1], (KX,), 0, XMODES), jax.random.fold_in(keys[1], 1), 0, XMODES - 1).astype(jnp.int32)
    kz_index = set_ends(jax.random.randint(keys[2], (KZ,), 0, KZ), jax.random.fold_in(keys[2], 1), 0, KZ - 1).astype(jnp.int32)
    helm_even = normal_values(keys[3], (NY // 2, NY // 2), (NY // 2) ** -0.5, 0.21875)
    helm_odd = normal_values(keys[4], (NY // 2, NY // 2), (NY // 2) ** -0.5, 0.21875)
    deriv_even = normal_values(keys[5], (NY // 2, NY // 2), (NY // 2) ** -0.5, 0.21875)
    deriv_odd = normal_values(keys[6], (NY // 2, NY // 2), (NY // 2) ** -0.5, 0.21875)
    return dict(velocity=velocity, kx_index=kx_index, kz_index=kz_index, helm_even=helm_even, helm_odd=helm_odd, deriv_even=deriv_even, deriv_odd=deriv_odd)


def slab_energy(plane):
    wide = plane.astype(jnp.float32)
    return jnp.sum(wide * wide)


def reference(velocity, kx_index, kz_index, helm_even, helm_odd, deriv_even, deriv_odd):
    half = NY // 2
    energy = jnp.sum(lax.map(slab_energy, jnp.moveaxis(velocity, 1, 0)))
    scale = jnp.float32(2.0 * KX * NY * KZ) / energy
    heven_mat = helm_even.astype(jnp.float32)
    hodd_mat = helm_odd.astype(jnp.float32)
    deven_mat = deriv_even.astype(jnp.float32)
    dodd_mat = deriv_odd.astype(jnp.float32)
    kz_sq = (kz_index.astype(jnp.float32) / KZ) ** 2

    def one_slab(inputs):
        plane, wave = inputs
        wide = plane.astype(jnp.float32)
        flip = wide[:, ::-1, :]
        even = ((wide[:, :half] + flip[:, :half]) * 0.5).astype(jnp.bfloat16)
        odd = ((wide[:, :half] - flip[:, :half]) * 0.5).astype(jnp.bfloat16)
        heven = jnp.einsum("cjz,ij->ciz", even.astype(jnp.float32), heven_mat).astype(jnp.bfloat16)
        hodd = jnp.einsum("cjz,ij->ciz", odd.astype(jnp.float32), hodd_mat).astype(jnp.bfloat16)
        he32 = heven.astype(jnp.float32)
        ho32 = hodd.astype(jnp.float32)
        dodd = jnp.einsum("cjz,ij->ciz", he32, deven_mat)
        deven = jnp.einsum("cjz,ij->ciz", ho32, dodd_mat)
        lines_u = jnp.concatenate([he32 + ho32, (he32 - ho32)[:, ::-1]], axis=1).astype(jnp.bfloat16)
        lines_d = jnp.concatenate([deven + dodd, (deven - dodd)[:, ::-1]], axis=1).astype(jnp.bfloat16)
        damp = 1.0 / (1.0 + 2.0 * ((wave.astype(jnp.float32) / XMODES) ** 2 + kz_sq))
        factor = scale * damp
        updated = (factor * lines_u.astype(jnp.float32)).astype(jnp.bfloat16)
        shear = (factor * lines_d.astype(jnp.float32)).astype(jnp.bfloat16)
        return updated, shear

    updated, shear = lax.map(one_slab, (jnp.moveaxis(velocity, 1, 0), kx_index))
    return jnp.moveaxis(updated, 0, 1), jnp.moveaxis(shear, 0, 1)
```

```python
import functools

import jax
import jax.numpy as jnp
from jax import lax
from jax.experimental import pallas as pl
from jax.experimental.pallas import tpu as pltpu
from jax.sharding import PartitionSpec as P

BF = jnp.bfloat16
F32 = jnp.float32
XMODES = 5120
LAG = 3
HBM = pl.BlockSpec(memory_space=pltpu.HBM)
SMEM = pl.BlockSpec(memory_space=pltpu.SMEM)
VMEM = pl.BlockSpec(memory_space=pltpu.VMEM)


def params():
    return pltpu.CompilerParams(vmem_limit_bytes=40 * 1024 * 1024)


def moved(nbytes):
    return pl.CostEstimate(flops=0, bytes_accessed=int(nbytes), transcendentals=0)


def operator_kernel(block, place_ref, rows_ref, cols_ref, he_ref, ho_ref, de_ref, do_ref, _, w_ref, source):
    h = he_ref.shape[0]
    p = rows_ref.shape[1]
    half = jnp.where(place_ref[2] == 1, -0.5, 0.5).astype(F32)

    @pl.loop(0, h // block)
    def _(b):
        at = pl.ds(pl.multiple_of(b * block, block), block)
        he, ho = he_ref[at, :].astype(F32), ho_ref[at, :].astype(F32)
        ge = jnp.dot(de_ref[at, :], he_ref[...], preferred_element_type=F32)
        go = jnp.dot(do_ref[at, :], ho_ref[...], preferred_element_type=F32)
        source[0, 0, at, :] = ((he + ho) * 0.5).astype(BF)
        source[1, 0, at, :] = ((he - ho) * 0.5).astype(BF)
        source[0, 1, at, :] = ((ge + go) * half).astype(BF)
        source[1, 1, at, :] = ((ge - go) * half).astype(BF)

    for side in range(2):
        from_col = lax.broadcasted_iota(jnp.int32, (h, h), 0)
        pick_cols = jnp.where(from_col == cols_ref[side : side + 1, :], 1.0, 0.0).astype(BF)

        @pl.loop(0, h // p)
        def _(b):
            at = pl.ds(pl.multiple_of(b * 2 * p, 2 * p), 2 * p)
            from_row = lax.broadcasted_iota(jnp.int32, (p, h), 1)
            pick_rows = jnp.where(from_row == rows_ref[b], 1.0, 0.0).astype(BF)
            picked = jnp.concatenate(
                [jnp.dot(pick_rows, source[side, f], preferred_element_type=F32) for f in range(2)], axis=0
            ).astype(BF)
            w_ref[at, side * h : (side + 1) * h] = jnp.dot(
                picked, pick_cols, preferred_element_type=F32
            ).astype(BF)


def operators(helm_even, helm_odd, deriv_even, deriv_odd, place, high, r, q, after):
    h = helm_even.shape[0]
    p = h // (2 * q)
    low = jnp.logical_not(high)
    block = h // 3 if h % 3 == 0 else h

    def order(part, member, plane, flipped):
        index = (part * q + member) * p + plane
        return jnp.where(flipped, h - 1 - index, index)

    index = lax.iota(jnp.int32, h)
    part, step, plane = index // (q * p), index // p % q, index % p
    to, came = (r + step) % q, (r - step + q) % q
    rows = order(jnp.where(low, part, 1 - part), to, plane, high)
    near = order(jnp.where(low, 1 - part, part), came, plane, high)
    far = order(jnp.where(low, part, 1 - part), came, plane, low)
    return pl.pallas_call(
        functools.partial(operator_kernel, block),
        in_specs=[SMEM] + [VMEM] * 6 + [HBM],
        out_specs=VMEM,
        out_shape=jax.ShapeDtypeStruct((2 * h, 2 * h), BF),
        scratch_shapes=[pltpu.VMEM((2, 2, h, h), BF)],
        compiler_params=params(),
        cost_estimate=pl.CostEstimate(flops=20 * h**3, bytes_accessed=16 * h * h, transcendentals=0),
        name="operators",
    )(place, rows.reshape(2 * q, p, 1), jnp.stack([near, far]), helm_even, helm_odd, deriv_even, deriv_odd, after)


def energy_kernel(v_ref, _, out_ref, total):
    i = pl.program_id(0)
    wide = v_ref[...].astype(F32)
    part = jnp.sum(wide * wide, axis=0)

    @pl.when(i == 0)
    def _():
        total[...] = part

    @pl.when(i > 0)
    def _():
        total[...] += part

    @pl.when(i == pl.num_programs(0) - 1)
    def _():
        out_ref[...] = jnp.sum(jnp.sum(total[...], axis=0, keepdims=True), axis=1, keepdims=True)


def energy_of(v, after):
    slabs, p, cols = v.shape
    block = 2 if slabs % 2 == 0 else 1
    return pl.pallas_call(
        energy_kernel,
        grid=(slabs // block,),
        in_specs=[pl.BlockSpec((block, p, cols), lambda i: (i, 0, 0)), HBM],
        out_specs=pl.BlockSpec((1, 1), lambda i: (0, 0)),
        out_shape=jax.ShapeDtypeStruct((1, 1), F32),
        scratch_shapes=[pltpu.VMEM((p, cols), F32)],
        compiler_params=params(),
        cost_estimate=moved(2 * v.size),
        name="energy",
    )(v, after)


def cut_kernel(pieces, place_ref, v_ref, _, *refs):
    outs, sems = refs[:-1], refs[-1]
    q, per = place_ref[3], place_ref[4]
    copies = []
    for i, (shift, t0, count, lane, width) in enumerate(pieces):
        first = lax.rem(place_ref[0] + shift, q) * per + t0
        copies.append(
            pltpu.make_async_copy(v_ref.at[pl.ds(first, count), :, pl.ds(lane, width)], outs[i], sems.at[i])
        )
    for copy in copies:
        copy.start()
    for copy in copies:
        copy.wait()


def cut(place, v, pieces, after):
    p = v.shape[1]
    shapes = [jax.ShapeDtypeStruct((count, p, width), BF) for _, _, count, _, width in pieces]
    return pl.pallas_call(
        functools.partial(cut_kernel, pieces),
        in_specs=[SMEM, HBM, HBM],
        out_specs=[HBM] * len(pieces),
        out_shape=shapes,
        scratch_shapes=[pltpu.SemaphoreType.DMA((len(pieces),))],
        compiler_params=params(),
        cost_estimate=moved(sum(4 * s.size for s in shapes)),
        name="cut",
    )(place, v, after)


class Step:
    def __init__(self, q, p, lanes, kx, product, result, operand, first=False):
        self.q, self.p, self.lanes, self.kx = q, p, lanes, kx
        self.product, self.result, self.operand, self.first = product, result, operand, first

    def kernel(self, *refs):
        q, p, lanes = self.q, self.p, self.lanes
        refs = list(refs)

        def take(count):
            taken = refs[:count]
            del refs[:count]
            return taken

        place, v = take(2)
        w, near, far = take(3) if self.product else (None,) * 3
        if self.result is not None:
            (factor,) = take(1)
            if not self.first:
                take(2)
            at_inner, at_outer = take(q), take(q)
        pieces = take(2 * q - 1) if self.operand is not None else []
        made = take(2 * q) if self.product else []
        updated, shear = take(2) if self.result is not None else (None, None)
        (later,) = take(1) if self.operand is not None else (None,)
        arrived, scaled, sems = refs
        r, inner, per = place[0], place[1] == 1, place[4]
        i = pl.program_id(0)
        last = 2 * q - 1 if self.product else 0

        def operand_copies():
            slab, lane, offset, lane_in = self.operand
            copies = [pltpu.make_async_copy(v.at[r * per + slab, :, pl.ds(lane, lanes)], later.at[pl.ds(0, p), :], sems.at[0])]
            for s, piece in enumerate(pieces):
                copies.append(
                    pltpu.make_async_copy(
                        piece.at[offset, :, pl.ds(lane_in, lanes)], later.at[pl.ds((s + 1) * p, p), :], sems.at[s + 1]
                    )
                )
            return copies

        def arriving(sources):
            return [pltpu.make_async_copy(sources[s], arrived.at[s], sems.at[2 * q + s]) for s in range(q)]

        def slab_of(s):
            return lax.rem(r - s + q, q) * per + self.result[0]

        def leaving():
            lane = self.result[1]
            copies = []
            for s in range(q):
                for f, out in enumerate((updated, shear)):
                    copies.append(
                        pltpu.make_async_copy(
                            scaled.at[s, pl.ds(f * p, p), :],
                            out.at[slab_of(s), :, pl.ds(lane, lanes)],
                            sems.at[3 * q + 2 * s + f],
                        )
                    )
            return copies

        @pl.when(i == 0)
        def _():
            if self.operand is not None:
                for copy in operand_copies():
                    copy.start()
            if self.result is not None:

                @pl.when(inner)
                def _():
                    for copy in arriving(at_inner):
                        copy.start()

                @pl.when(jnp.logical_not(inner))
                def _():
                    for copy in arriving(at_outer):
                        copy.start()

        if self.product:
            half = near.shape[0]
            acc = jnp.dot(w[:, :half], near[...], preferred_element_type=F32)
            acc += jnp.dot(w[:, half:], far[...], preferred_element_type=F32)
            acc = acc.astype(BF)
            for k in range(2 * q):

                @pl.when(i == k)
                def _():
                    made[k][...] = acc

        if self.result is not None:

            @pl.when(i == 0)
            def _():
                for copy in arriving(at_inner):
                    copy.wait()
                for s in range(q):
                    k = lax.rem(slab_of(s), self.kx)
                    f = factor[k, :, pl.ds(self.result[1], lanes)]
                    scaled[s] = (arrived[s].astype(F32) * f).astype(BF)
                for copy in leaving():
                    copy.start()

        @pl.when(i == last)
        def _():
            if self.result is not None:
                for copy in leaving():
                    copy.wait()
            if self.operand is not None:
                for copy in operand_copies():
                    copy.wait()

    def call(self, place, v, product_args=(), result_args=(), operand_args=()):
        q, p, lanes = self.q, self.p, self.lanes
        in_specs, args = [SMEM, HBM], [place, v]
        out_specs, out_shape, aliases = [], [], {}
        flops = nbytes = 0
        if self.product:
            w, near, far = product_args
            depth = w.shape[1]
            in_specs += [
                pl.BlockSpec((2 * p, depth), lambda i: (i, 0)),
                pl.BlockSpec(near.shape, lambda i: (0, 0)),
                pl.BlockSpec(near.shape, lambda i: (0, 0)),
            ]
            args += list(product_args)
            out_specs += [pl.BlockSpec((2 * p, lanes), lambda i: (0, 0))] * (2 * q)
            out_shape += [jax.ShapeDtypeStruct((2 * p, lanes), BF)] * (2 * q)
            flops += 2 * depth * depth * lanes
            nbytes += 2 * depth * (depth + 2 * lanes)
        if self.result is not None:
            factor, updated, shear, at_inner, at_outer = result_args
            before = [] if self.first else [updated, shear]
            if before:
                aliases = {len(args) + 1: len(out_shape), len(args) + 2: len(out_shape) + 1}
            in_specs += [pl.BlockSpec(factor.shape, lambda i: (0, 0, 0))] + [HBM] * (len(before) + 2 * q)
            args += [factor, *before, *at_inner, *at_outer]
            out_specs += [HBM] * 2
            out_shape += [jax.ShapeDtypeStruct(v.shape, BF)] * 2
            nbytes += 8 * q * p * lanes
        if self.operand is not None:
            in_specs += [HBM] * len(operand_args)
            args += list(operand_args)
            out_specs += [HBM]
            out_shape += [jax.ShapeDtypeStruct((2 * q * p, lanes), BF)]
            nbytes += 8 * q * p * lanes
        return list(
            pl.pallas_call(
                self.kernel,
                grid=(2 * q if self.product else 1,),
                in_specs=in_specs,
                out_specs=out_specs,
                out_shape=out_shape,
                scratch_shapes=[
                    pltpu.VMEM((q, 2 * p, lanes), BF),
                    pltpu.VMEM((q, 2 * p, lanes), BF),
                    pltpu.SemaphoreType.DMA((5 * q,)),
                ],
                input_output_aliases=aliases,
                compiler_params=params(),
                cost_estimate=pl.CostEstimate(flops=flops, bytes_accessed=nbytes, transcendentals=0),
                name="step",
            )(*args)
        )


def doubling_sum(x, axis, n):
    if n & (n - 1):
        return lax.psum(x, axis)
    step = 1
    while step < n:
        x = x + lax.ppermute(x, axis, [(i, i ^ step) for i in range(n)])
        step *= 2
    return x


def local(sizes, kz, velocity, kx_index, kz_index, helm_even, helm_odd, deriv_even, deriv_odd):
    n, n_span = sizes
    c, kx, p, cols = velocity.shape
    q = n // 4
    slabs = c * kx
    per = slabs // q
    lanes = cols // 2
    v = velocity.reshape(slabs, p, cols)
    me = lax.axis_index("wall")
    quarter, r = me // q, me % q
    high = quarter >= 2
    inner = (quarter == 1) | (quarter == 2)
    place = jnp.stack([r, inner.astype(jnp.int32), high.astype(jnp.int32), jnp.int32(q), jnp.int32(per)]).astype(jnp.int32)

    def pairs(quarters, shift=0):
        return [(a * q + j, b * q + (j + shift) % q) for a, b in quarters for j in range(q)]

    own = [(a, a) for a in range(4)]
    own_inner = [(1, 1), (2, 2)]
    to_inner, to_outer, middle = [(0, 1), (3, 2)], [(1, 0), (2, 3)], [(1, 2), (2, 1)]

    def send(x, quarters, shift=0):
        return lax.ppermute(x, "wall", pairs(quarters, shift))

    chunks = [(t, lane) for t in range(per) for lane in (0, lanes)]
    runs = [(0, 1, 0, lanes), (0, 1, lanes, lanes)]
    t, count = 1, 1
    while t < per:
        count = min(count, per - t)
        runs.append((t, count, 0, cols))
        t, count = t + count, 2 * count

    gathered = []

    def gather(cuts, direct):
        within = [send(cuts[s], own, s) for s in range(1, q)]
        outer = [send(cuts[0], to_inner)]
        for s in range(1, q):
            outer.append(send(cuts[s], to_inner, s) if direct else send(within[s - 1], to_inner))
        gathered.append(within + outer)

    def operand(i):
        t, lane = chunks[i]
        for j, (t0, count, lane0, width) in enumerate(runs):
            if t0 <= t < t0 + count and lane0 <= lane < lane0 + width:
                return (t, lane, t - t0, lane - lane0), gathered[j]

    total = len(chunks)
    ahead = min(2, total)
    near, far, results = {}, {}, {}
    for i in range(ahead):
        gather(cut(place, v, [(s, *runs[i]) for s in range(q)], place), i == 0)
        where, args = operand(i)
        (near[i],) = Step(q, p, lanes, kx, False, None, where).call(place, v, operand_args=args)
        far[i] = send(near[i], middle)
    if runs[2:]:
        cuts = cut(place, v, [(s, *run) for run in runs[2:] for s in range(q)], near[0])
        for i in range(len(runs) - 2):
            gather(cuts[i * q : (i + 1) * q], False)

    w = operators(helm_even, helm_odd, deriv_even, deriv_odd, place, high, r, q, near[0])
    energy = energy_of(v, near[0])
    energy = doubling_sum(doubling_sum(energy, "wall", n), "span", n_span)
    scale = jnp.float32(float(c * kx * n * p * cols * n_span)) / energy[0, 0]
    kx_sq = (kx_index.astype(F32) / XMODES) ** 2
    kz_sq = (kz_index.astype(F32) / kz) ** 2
    factor = scale * (1.0 / (1.0 + 2.0 * (kx_sq[:, None, None] + kz_sq[None, None, :])))

    updated = shear = None
    for i in range(total + LAG):
        done, late = i - LAG, i + ahead
        product = i < total
        where, operand_args = operand(late) if late < total else (None, ())
        step = Step(q, p, lanes, kx, product, chunks[done] if done >= 0 else None, where, done == 0)
        out = step.call(
            place,
            v,
            (w, near[i], far[i]) if product else (),
            (factor, updated, shear, *results.pop(done)) if done >= 0 else (),
            operand_args,
        )
        if late < total:
            near[late] = out.pop()
            far[late] = send(near[late], middle)
        if done >= 0:
            shear = out.pop()
            updated = out.pop()
        if product:
            outer, in_place = out[:q], out[q:]
            at_outer = [send(outer[s], to_outer, s) for s in range(q)]
            at_inner = in_place[:1] + [send(in_place[s], own_inner, s) for s in range(1, q)]
            results[i] = (at_inner, at_outer)
    return updated.reshape(velocity.shape), shear.reshape(velocity.shape)


def solution(mesh):
    sizes = (mesh.shape["wall"], mesh.shape["span"])

    def whole(velocity, *rest):
        body = functools.partial(local, sizes, velocity.shape[3])
        in_specs = (P(None, None, "wall", "span"), P(), P("span"), P(), P(), P(), P())
        out_specs = (P(None, None, "wall", "span"), P(None, None, "wall", "span"))
        return jax.shard_map(body, mesh=mesh, in_specs=in_specs, out_specs=out_specs, check_vma=False)(velocity, *rest)

    return whole
```

```python
import functools

import jax
import jax.numpy as jnp
from jax import lax
from jax.experimental import pallas as pl
from jax.experimental.pallas import tpu as pltpu
from jax.sharding import PartitionSpec as P

BF = jnp.bfloat16
F32 = jnp.float32
XMODES = 5120
LAG = 3
HBM = pl.BlockSpec(memory_space=pltpu.HBM)
SMEM = pl.BlockSpec(memory_space=pltpu.SMEM)
VMEM = pl.BlockSpec(memory_space=pltpu.VMEM)


def params(mib=24):
    return pltpu.CompilerParams(vmem_limit_bytes=mib * 1024 * 1024)


def cost(flops, nbytes):
    return pl.CostEstimate(flops=int(flops), bytes_accessed=int(nbytes), transcendentals=0)


def operator_kernel(block, place_ref, rows_ref, cols_ref, *refs):
    given, (w_ref, held, source, sems) = refs[:4], refs[-4:]
    h = rows_ref.shape[0]
    p = block
    copies = [pltpu.make_async_copy(x, held.at[i], sems.at[i]) for i, x in enumerate(given)]
    for copy in copies:
        copy.start()
    half = jnp.where(place_ref[2] == 1, -0.5, 0.5).astype(F32)
    from_row = lax.broadcasted_iota(jnp.int32, (h, h), 1)
    pick_rows = jnp.where(from_row == rows_ref[...], 1.0, 0.0).astype(BF)

    def product(a, b):
        return jnp.dot(a, b, preferred_element_type=F32)

    def combine(field, even, odd, factor):
        source[0, field] = product(pick_rows, ((even + odd) * factor).astype(BF)).astype(BF)
        source[1, field] = product(pick_rows, ((even - odd) * factor).astype(BF)).astype(BF)

    copies[0].wait()
    copies[1].wait()
    combine(0, held[0].astype(F32), held[1].astype(F32), 0.5)
    copies[2].wait()
    copies[3].wait()
    combine(1, product(held[2], held[0]), product(held[3], held[1]), half)
    for side in range(2):
        from_col = lax.broadcasted_iota(jnp.int32, (h, h), 0)
        pick_cols = jnp.where(from_col == cols_ref[side : side + 1, :], 1.0, 0.0).astype(BF)
        for field in range(2):
            picked = product(source[side, field], pick_cols)
            for s in range(h // p):
                at = (2 * s + field) * p
                w_ref[at : at + p, side * h : (side + 1) * h] = picked[s * p : (s + 1) * p].astype(BF)


def operators(helm_even, helm_odd, deriv_even, deriv_odd, place, high, r, q, after):
    h = helm_even.shape[0]
    p = h // (2 * q)
    low = jnp.logical_not(high)

    def order(part, member, plane, flipped):
        index = (part * q + member) * p + plane
        return jnp.where(flipped, h - 1 - index, index)

    index = lax.iota(jnp.int32, h)
    part, step, plane = index // (q * p), index // p % q, index % p
    to, came = (r + step) % q, (r - step + q) % q
    rows = order(jnp.where(low, part, 1 - part), to, plane, high)
    near = order(jnp.where(low, 1 - part, part), came, plane, high)
    far = order(jnp.where(low, part, 1 - part), came, plane, low)
    return pl.pallas_call(
        functools.partial(operator_kernel, p),
        in_specs=[SMEM, VMEM, VMEM] + [HBM] * (4 + len(after)),
        out_specs=VMEM,
        out_shape=jax.ShapeDtypeStruct((2 * h, 2 * h), BF),
        scratch_shapes=[pltpu.VMEM((4, h, h), BF), pltpu.VMEM((2, 2, h, h), BF), pltpu.SemaphoreType.DMA((4,))],
        compiler_params=params() if p % 16 == 0 else params(48),
        cost_estimate=cost(20 * h**3, 16 * h * h),
        name="operators",
    )(place, rows[:, None], jnp.stack([near, far]), helm_even, helm_odd, deriv_even, deriv_odd, *after)


def energy_kernel(v_ref, out_ref, total):
    i = pl.program_id(0)
    wide = v_ref[...].astype(F32)
    part = jnp.sum((wide * wide).reshape(-1, *total.shape), axis=0)

    @pl.when(i == 0)
    def _():
        total[...] = part

    @pl.when(i > 0)
    def _():
        total[...] += part

    @pl.when(i == pl.num_programs(0) - 1)
    def _():
        out_ref[...] = jnp.sum(jnp.sum(total[...], axis=0, keepdims=True), axis=1, keepdims=True)


def energy_of(v):
    slabs, p, cols = v.shape
    block = 2 if slabs % 2 == 0 else 1
    return pl.pallas_call(
        energy_kernel,
        grid=(slabs // block,),
        in_specs=[pl.BlockSpec((block * p, cols), lambda i: (i, 0))],
        out_specs=pl.BlockSpec((1, 1), lambda i: (0, 0)),
        out_shape=jax.ShapeDtypeStruct((1, 1), F32),
        scratch_shapes=[pltpu.VMEM((8, cols), F32)],
        compiler_params=params(),
        cost_estimate=cost(0, 2 * v.size),
        name="energy",
    )(v.reshape(slabs * p, cols))


def cut_kernel(pieces, place_ref, v_ref, *refs):
    outs, stages, (sems,) = refs[-2 * len(pieces) - 1 : -len(pieces) - 1], refs[-len(pieces) - 1 : -1], refs[-1:]
    q, per = place_ref[3], place_ref[4]
    read, write = [], []
    for i, (shift, t0, count, lane, width) in enumerate(pieces):
        first = lax.rem(place_ref[0] + shift, q) * per + t0
        source = v_ref.at[pl.ds(first, count), :, pl.ds(lane, width)]
        read.append(pltpu.make_async_copy(source, stages[i], sems.at[0, i]))
        write.append(pltpu.make_async_copy(stages[i], outs[i], sems.at[1, i]))
    for copy in read:
        copy.start()
    for i in range(len(pieces)):
        read[i].wait()
        write[i].start()
    for copy in write:
        copy.wait()


def cut(place, v, pieces, after, mib=24):
    p = v.shape[1]
    shapes = [(count, p, width) for _, _, count, _, width in pieces]
    return pl.pallas_call(
        functools.partial(cut_kernel, pieces),
        in_specs=[SMEM, HBM] + [HBM] * len(after),
        out_specs=[HBM] * len(pieces),
        out_shape=[jax.ShapeDtypeStruct(shape, BF) for shape in shapes],
        scratch_shapes=[pltpu.VMEM(shape, BF) for shape in shapes] + [pltpu.SemaphoreType.DMA((2, len(pieces)))],
        compiler_params=params(mib),
        cost_estimate=cost(0, 4 * p * sum(count * width for _, _, count, _, width in pieces)),
        name="cut",
    )(place, v, *after)


class Step:
    def __init__(self, q, p, lanes, kx, product, result, operand, first=False):
        self.q, self.p, self.lanes, self.kx = q, p, lanes, kx
        self.product, self.result, self.operand, self.first = product, result, operand, first

    def kernel(self, *refs):
        q, p, lanes = self.q, self.p, self.lanes
        refs = list(refs)

        def take(count):
            taken = refs[:count]
            del refs[:count]
            return taken

        take(self.n_after)
        (place,) = take(1)
        w, near, far = take(3) if self.product else (None,) * 3
        if self.result is not None:
            (factor,) = take(1)
            if not self.first:
                take(2)
            at_inner, at_outer = take(q), take(q)
        pieces = take(2 * q) if self.operand is not None else []
        made = take(2 * q) if self.product else []
        updated, shear = take(2) if self.result is not None else (None, None)
        (later,) = take(1) if self.operand is not None else (None,)
        arrived, scaled, staged, sems = refs
        r, inner, per = place[0], place[1] == 1, place[4]
        i = pl.program_id(0)
        last = 2 * q - 1 if self.product else 0

        def operand_copies():
            offset, lane = self.operand
            sources = [piece.at[offset, :, pl.ds(lane, lanes)] for piece in pieces]
            return [
                pltpu.make_async_copy(source, staged.at[pl.ds(s * p, p), :], sems.at[s])
                for s, source in enumerate(sources)
            ]

        def operand_out():
            return pltpu.make_async_copy(staged, later, sems.at[5 * q])

        def arriving(sources):
            return [pltpu.make_async_copy(sources[s], arrived.at[s], sems.at[2 * q + s]) for s in range(q)]

        def slab_of(s):
            return lax.rem(r - s + q, q) * per + self.result[0]

        def leaving():
            lane = self.result[1]
            copies = []
            for s in range(q):
                for f, out in enumerate((updated, shear)):
                    copies.append(
                        pltpu.make_async_copy(
                            scaled.at[s, pl.ds(f * p, p), :],
                            out.at[slab_of(s), :, pl.ds(lane, lanes)],
                            sems.at[3 * q + 2 * s + f],
                        )
                    )
            return copies

        @pl.when(i == 0)
        def _():
            if self.operand is not None:
                for copy in operand_copies():
                    copy.start()
            if self.result is not None:

                @pl.when(inner)
                def _():
                    for copy in arriving(at_inner):
                        copy.start()

                @pl.when(jnp.logical_not(inner))
                def _():
                    for copy in arriving(at_outer):
                        copy.start()

        if self.product:
            half = near.shape[0]
            acc = jnp.dot(w[:, :half], near[...], preferred_element_type=F32)
            acc += jnp.dot(w[:, half:], far[...], preferred_element_type=F32)
            acc = acc.astype(BF)
            for k in range(2 * q):

                @pl.when(i == k)
                def _():
                    made[k][...] = acc

        if self.result is not None:

            @pl.when(i == 0)
            def _():
                for copy in arriving(at_inner):
                    copy.wait()
                for s in range(q):
                    k = lax.rem(slab_of(s), self.kx)
                    f = factor[k, :, pl.ds(self.result[1], lanes)]
                    scaled[s] = (arrived[s].astype(F32) * f).astype(BF)
                for copy in leaving():
                    copy.start()

        if self.operand is not None:

            @pl.when(i == min(1, last))
            def _():
                for copy in operand_copies():
                    copy.wait()
                operand_out().start()

        @pl.when(i == last)
        def _():
            if self.result is not None:
                for copy in leaving():
                    copy.wait()
            if self.operand is not None:
                operand_out().wait()

    def call(self, place, shape, product_args=(), result_args=(), operand_args=(), after=()):
        self.n_after = len(after)
        q, p, lanes = self.q, self.p, self.lanes
        in_specs, args = [HBM] * len(after) + [SMEM], [*after, place]
        out_specs, out_shape, aliases = [], [], {}
        flops = nbytes = 0
        if self.product:
            w, near, far = product_args
            depth = w.shape[1]
            in_specs += [
                pl.BlockSpec((2 * p, depth), lambda i: (i, 0)),
                pl.BlockSpec(near.shape, lambda i: (0, 0)),
                pl.BlockSpec(near.shape, lambda i: (0, 0)),
            ]
            args += list(product_args)
            flops += 2 * depth * depth * lanes
            nbytes += 2 * depth * (depth + 2 * lanes)
            out_specs += [pl.BlockSpec((2 * p, lanes), lambda i: (0, 0))] * (2 * q)
            out_shape += [jax.ShapeDtypeStruct((2 * p, lanes), BF)] * (2 * q)
        if self.result is not None:
            factor, updated, shear, at_inner, at_outer = result_args
            before = [] if self.first else [updated, shear]
            if before:
                aliases = {len(args) + 1: len(out_shape), len(args) + 2: len(out_shape) + 1}
            in_specs += [pl.BlockSpec(factor.shape, lambda i: (0, 0, 0))] + [HBM] * (len(before) + 2 * q)
            args += [factor, *before, *at_inner, *at_outer]
            nbytes += 8 * q * p * lanes
            out_specs += [HBM] * 2
            out_shape += [jax.ShapeDtypeStruct(shape, BF)] * 2
        if self.operand is not None:
            in_specs += [HBM] * len(operand_args)
            args += list(operand_args)
            nbytes += 8 * q * p * lanes
            out_specs += [HBM]
            out_shape += [jax.ShapeDtypeStruct((2 * q * p, lanes), BF)]
        return list(
            pl.pallas_call(
                self.kernel,
                grid=(2 * q if self.product else 1,),
                in_specs=in_specs,
                out_specs=out_specs,
                out_shape=out_shape,
                scratch_shapes=[
                    pltpu.VMEM((q, 2 * p, lanes), BF),
                    pltpu.VMEM((q, 2 * p, lanes), BF),
                    pltpu.VMEM((2 * q * p, lanes), BF),
                    pltpu.SemaphoreType.DMA((5 * q + 1,)),
                ],
                input_output_aliases=aliases,
                compiler_params=params(),
                cost_estimate=cost(flops, nbytes),
                name="step",
            )(*args)
        )


def rounds(axis, n, first=()):
    if n & (n - 1):
        return [lambda x: lax.psum(x, axis)]
    steps = sorted((1 << k for k in range(n.bit_length() - 1)), key=lambda step: (step not in first, -step))
    return [lambda x, step=step: x + lax.ppermute(x, axis, [(i, i ^ step) for i in range(n)]) for step in steps]


def local(sizes, kz, velocity, kx_index, kz_index, helm_even, helm_odd, deriv_even, deriv_odd):
    n, n_span = sizes
    c, kx, p, cols = velocity.shape
    q = n // 4
    slabs = c * kx
    per = slabs // q
    lanes = cols // 2
    v = velocity.reshape(slabs, p, cols)
    me = lax.axis_index("wall")
    quarter, r = me // q, me % q
    high = quarter >= 2
    inner = (quarter == 1) | (quarter == 2)
    place = jnp.stack([r, inner.astype(jnp.int32), high.astype(jnp.int32), jnp.int32(q), jnp.int32(per)]).astype(jnp.int32)

    def pairs(quarters, shift=0):
        return [(a * q + j, b * q + (j + shift) % q) for a, b in quarters for j in range(q)]

    own = [(a, a) for a in range(4)]
    own_inner = [(1, 1), (2, 2)]
    to_inner, to_outer, middle = [(0, 1), (3, 2)], [(1, 0), (2, 3)], [(1, 2), (2, 1)]

    def send(x, quarters, shift=0):
        return lax.ppermute(x, "wall", pairs(quarters, shift))

    chunks = [(t, lane) for t in range(per) for lane in (0, lanes)]
    runs = [(t, 1) for t in range(min(2, per))] + [(t, min(2, per - t)) for t in range(2, per, 2)]

    gathered = []

    def gather(cuts, direct):
        within = [send(cuts[s], own, s) for s in range(1, q)]
        outer = [send(cuts[0], to_inner)]
        for s in range(1, q):
            outer.append(send(cuts[s], to_inner, s) if direct else send(within[s - 1], to_inner))
        gathered.append([cuts[0], *within, *outer])

    def operand(i):
        t, lane = chunks[i]
        j = next(j for j, (t0, count) in enumerate(runs) if t0 <= t < t0 + count)
        return (t - runs[j][0], lane), gathered[j]

    def pieces(j):
        return [(s, *runs[j], 0, cols) for s in range(q)]

    total = len(chunks)
    ahead = 2
    near, far, results = {}, {}, {}
    gather(cut(place, v, pieces(0), (), 56), True)
    energy = energy_of(v)
    wall_rounds = rounds("wall", n, (n // 2, n // 4))
    for add in wall_rounds[:2]:
        energy = add(energy)
    w = operators(helm_even, helm_odd, deriv_even, deriv_odd, place, high, r, q, ())

    def make_operand(i, after):
        where, args = operand(i)
        (near[i],) = Step(q, p, lanes, kx, False, None, where).call(place, v.shape, operand_args=args, after=after)
        far[i] = send(near[i], middle)

    make_operand(0, [w, energy])
    make_operand(1, [])
    if len(runs) > 1:
        gather(cut(place, v, pieces(1), [near[0]]), True)
    energy, _ = lax.optimization_barrier((energy, near[1]))
    for add in wall_rounds[2:] + rounds("span", n_span):
        energy = add(energy)
    asked, wanted = {}, {0: [energy]}
    for j in range(2, len(runs)):
        asked.setdefault(max(0, 2 * runs[j][0] - ahead - 4), []).append(j)

    def ask(i):
        for j in asked.get(i, []):
            gather(cut(place, v, pieces(j), [near[max(near)]]), False)
            use = 2 * runs[j][0] - ahead
            lines = gathered[-1]
            wanted.setdefault(max(use - 2, i + 1), []).extend(lines[1:q])
            wanted.setdefault(max(use - 1, i + 2), []).extend(lines[q : q + 1])

    def factor_of(energy):
        scale = jnp.float32(float(c * kx * n * p * cols * n_span)) / energy[0, 0]
        kx_sq = (kx_index.astype(F32) / XMODES) ** 2
        kz_sq = (kz_index.astype(F32) / kz) ** 2
        return scale * (1.0 / (1.0 + 2.0 * (kx_sq[:, None, None] + kz_sq[None, None, :])))

    factor = factor_of(energy)
    updated = shear = None
    for i in range(total + LAG):
        done, late = i - LAG, i + ahead
        product = i < total
        where, operand_args = operand(late) if 0 < i and late < total else (None, ())
        step = Step(q, p, lanes, kx, product, chunks[done] if done >= 0 else None, where, done == 0)
        out = step.call(
            place,
            v.shape,
            (w, near[i], far[i]) if product else (),
            (factor, updated, shear, *results.pop(done)) if done >= 0 else (),
            operand_args,
            wanted.pop(i, []),
        )
        if 0 < i and late < total:
            near[late] = out.pop()
            far[late] = send(near[late], middle)
        if done >= 0:
            shear = out.pop()
            updated = out.pop()
        if product:
            outer, in_place = out[:q], out[q:]
            at_outer = [send(outer[s], to_outer, s) for s in range(q)]
            at_inner = in_place[:1] + [send(in_place[s], own_inner, s) for s in range(1, q)]
            results[i] = (at_inner, at_outer)
            wanted.setdefault(i + 2, []).extend(at_inner[1:] + at_outer)
            if i == 0 and late < total:
                make_operand(late, out[q : q + 1])
            ask(i)
    return updated.reshape(velocity.shape), shear.reshape(velocity.shape)


def solution(mesh):
    sizes = (mesh.shape["wall"], mesh.shape["span"])

    def whole(velocity, *rest):
        body = functools.partial(local, sizes, velocity.shape[3])
        in_specs = (P(None, None, "wall", "span"), P(), P("span"), P(), P(), P(), P())
        out_specs = (P(None, None, "wall", "span"), P(None, None, "wall", "span"))
        return jax.shard_map(body, mesh=mesh, in_specs=in_specs, out_specs=out_specs, check_vma=False)(velocity, *rest)

    return whole
```

```python
import functools

import jax
import jax.numpy as jnp
from jax import lax
from jax.experimental import pallas as pl
from jax.experimental.pallas import tpu as pltpu
from jax.sharding import PartitionSpec as P

BF = jnp.bfloat16
F32 = jnp.float32
XMODES = 5120
HOP = 2
LAG = 2 * HOP
HBM = pl.BlockSpec(memory_space=pltpu.HBM)
SMEM = pl.BlockSpec(memory_space=pltpu.SMEM)
VMEM = pl.BlockSpec(memory_space=pltpu.VMEM)


def params(mib=24):
    return pltpu.CompilerParams(vmem_limit_bytes=mib * 1024 * 1024)


def cost(flops, nbytes):
    return pl.CostEstimate(flops=int(flops), bytes_accessed=int(nbytes), transcendentals=0)


def operator_kernel(block, place_ref, rows_ref, cols_ref, *refs):
    given, (w_ref, held, source, sems) = refs[:4], refs[-4:]
    h = rows_ref.shape[0]
    p = block
    copies = [pltpu.make_async_copy(x, held.at[i], sems.at[i]) for i, x in enumerate(given)]
    for copy in copies:
        copy.start()
    half = jnp.where(place_ref[2] == 1, -0.5, 0.5).astype(F32)
    from_row = lax.broadcasted_iota(jnp.int32, (h, h), 1)
    pick_rows = jnp.where(from_row == rows_ref[...], 1.0, 0.0).astype(BF)

    def product(a, b):
        return jnp.dot(a, b, preferred_element_type=F32)

    def combine(field, even, odd, factor):
        source[0, field] = product(pick_rows, ((even + odd) * factor).astype(BF)).astype(BF)
        source[1, field] = product(pick_rows, ((even - odd) * factor).astype(BF)).astype(BF)

    copies[0].wait()
    copies[1].wait()
    combine(0, held[0].astype(F32), held[1].astype(F32), 0.5)
    copies[2].wait()
    copies[3].wait()
    combine(1, product(held[2], held[0]), product(held[3], held[1]), half)
    for side in range(2):
        from_col = lax.broadcasted_iota(jnp.int32, (h, h), 0)
        pick_cols = jnp.where(from_col == cols_ref[side : side + 1, :], 1.0, 0.0).astype(BF)
        for field in range(2):
            picked = product(source[side, field], pick_cols)
            for s in range(h // p):
                at = (2 * s + field) * p
                w_ref[at : at + p, side * h : (side + 1) * h] = picked[s * p : (s + 1) * p].astype(BF)


def operators(helm_even, helm_odd, deriv_even, deriv_odd, place, high, r, q, after):
    h = helm_even.shape[0]
    p = h // (2 * q)
    low = jnp.logical_not(high)

    def order(part, member, plane, flipped):
        index = (part * q + member) * p + plane
        return jnp.where(flipped, h - 1 - index, index)

    index = lax.iota(jnp.int32, h)
    part, step, plane = index // (q * p), index // p % q, index % p
    to, came = (r + step) % q, (r - step + q) % q
    rows = order(jnp.where(low, part, 1 - part), to, plane, high)
    near = order(jnp.where(low, 1 - part, part), came, plane, high)
    far = order(jnp.where(low, part, 1 - part), came, plane, low)
    return pl.pallas_call(
        functools.partial(operator_kernel, p),
        in_specs=[SMEM, VMEM, VMEM] + [HBM] * (4 + len(after)),
        out_specs=VMEM,
        out_shape=jax.ShapeDtypeStruct((2 * h, 2 * h), BF),
        scratch_shapes=[pltpu.VMEM((4, h, h), BF), pltpu.VMEM((2, 2, h, h), BF), pltpu.SemaphoreType.DMA((4,))],
        compiler_params=params() if p % 16 == 0 else params(48),
        cost_estimate=cost(20 * h**3, 16 * h * h),
        name="operators",
    )(place, rows[:, None], jnp.stack([near, far]), helm_even, helm_odd, deriv_even, deriv_odd, *after)


def energy_kernel(v_ref, out_ref, total):
    i = pl.program_id(0)
    wide = v_ref[...].astype(F32)
    part = jnp.sum((wide * wide).reshape(-1, *total.shape), axis=0)

    @pl.when(i == 0)
    def _():
        total[...] = part

    @pl.when(i > 0)
    def _():
        total[...] += part

    @pl.when(i == pl.num_programs(0) - 1)
    def _():
        out_ref[...] = jnp.sum(jnp.sum(total[...], axis=0, keepdims=True), axis=1, keepdims=True)


def energy_of(v):
    slabs, p, cols = v.shape
    block = 2 if slabs % 2 == 0 else 1
    return pl.pallas_call(
        energy_kernel,
        grid=(slabs // block,),
        in_specs=[pl.BlockSpec((block * p, cols), lambda i: (i, 0))],
        out_specs=pl.BlockSpec((1, 1), lambda i: (0, 0)),
        out_shape=jax.ShapeDtypeStruct((1, 1), F32),
        scratch_shapes=[pltpu.VMEM((8, cols), F32)],
        compiler_params=params(),
        cost_estimate=cost(0, 2 * v.size),
        name="energy",
    )(v.reshape(slabs * p, cols))


def cut_kernel(pieces, place_ref, v_ref, *refs):
    outs, stages, (sems,) = refs[-2 * len(pieces) - 1 : -len(pieces) - 1], refs[-len(pieces) - 1 : -1], refs[-1:]
    q, per = place_ref[3], place_ref[4]
    read, write = [], []
    for i, (shift, t0, count, lane, width) in enumerate(pieces):
        first = lax.rem(place_ref[0] + shift, q) * per + t0
        source = v_ref.at[pl.ds(first, count), :, pl.ds(lane, width)]
        read.append(pltpu.make_async_copy(source, stages[i], sems.at[0, i]))
        write.append(pltpu.make_async_copy(stages[i], outs[i], sems.at[1, i]))
    for copy in read:
        copy.start()
    for i in range(len(pieces)):
        read[i].wait()
        write[i].start()
    for copy in write:
        copy.wait()


def cut(place, v, pieces, after, mib=24):
    p = v.shape[1]
    shapes = [(count, p, width) for _, _, count, _, width in pieces]
    return pl.pallas_call(
        functools.partial(cut_kernel, pieces),
        in_specs=[SMEM, HBM] + [HBM] * len(after),
        out_specs=[HBM] * len(pieces),
        out_shape=[jax.ShapeDtypeStruct(shape, BF) for shape in shapes],
        scratch_shapes=[pltpu.VMEM(shape, BF) for shape in shapes] + [pltpu.SemaphoreType.DMA((2, len(pieces)))],
        compiler_params=params(mib),
        cost_estimate=cost(0, 4 * p * sum(count * width for _, _, count, _, width in pieces)),
        name="cut",
    )(place, v, *after)


def pass_on_kernel(n, *refs):
    given, made, (sems,) = refs[:n], refs[-n - 1 : -1], refs[-1:]
    copies = [pltpu.make_async_copy(given[i], made[i], sems.at[i]) for i in range(n)]
    for copy in copies:
        copy.start()
    for copy in copies:
        copy.wait()


def pass_on(arrays, after):
    n = len(arrays)
    return pl.pallas_call(
        functools.partial(pass_on_kernel, n),
        in_specs=[VMEM] * n + [HBM] * len(after),
        out_specs=[HBM] * n,
        out_shape=[jax.ShapeDtypeStruct(x.shape, BF) for x in arrays],
        scratch_shapes=[pltpu.SemaphoreType.DMA((n,))],
        compiler_params=params(),
        cost_estimate=cost(0, 4 * sum(x.size for x in arrays)),
        name="pass_on",
    )(*arrays, *after)


class Step:
    def __init__(self, sizes, place, v):
        self.q, self.p, self.lanes, self.kx = sizes
        self.place, self.v = place, v
        self.operands = [place, v]
        self.sems = 0

    def block(self, array, row, count, lane=0, lead=None):
        known = [i for i, x in enumerate(self.operands) if x is array]
        if not known:
            self.operands.append(array)
        k = known[0] if known else len(self.operands) - 1

        def ref(refs):
            rows, cols = pl.ds(row, count), pl.ds(lane, self.lanes)
            return refs[k].at[rows, cols] if lead is None else refs[k].at[lead, rows, cols]

        return ref, count

    def planes(self, shift, chunk):
        slab, lane = chunk

        def ref(refs):
            first = lax.rem(refs[0][0] + shift, self.q) * refs[0][4] + slab
            return refs[1].at[first, :, pl.ds(lane, self.lanes)]

        return ref, self.p

    def copies(self, refs, blocks, target, sems, first):
        made, row = [], 0
        for i, (ref, count) in enumerate(blocks):
            made.append(pltpu.make_async_copy(ref(refs), target.at[pl.ds(row, count), :], sems.at[first + i]))
            row += count
        return made

    def call(self, product=None, near=(), lines=(), relay=(), ahead=(), results=(), into=None, split=False, after=()):
        q, p, lanes = self.q, self.p, self.lanes
        n_data = len(self.operands)
        steps = 2 * q if product else 1
        in_specs = [SMEM] + [HBM] * (n_data - 1)
        args = list(self.operands)
        flops = nbytes = 0
        if product:
            w = product[0]
            depth = w.shape[1]
            in_specs += [pl.BlockSpec((2 * p, depth), lambda i: (i, 0))]
            in_specs += [pl.BlockSpec(product[1].shape, lambda i: (0, 0))] * 2
            args += list(product)
            flops += 2 * depth * depth * lanes
            nbytes += 2 * depth * (depth + 2 * lanes)
        out_specs, out_shape, aliases = [], [], {}

        def out(shape, spec=HBM):
            out_specs.append(spec)
            out_shape.append(jax.ShapeDtypeStruct(shape, BF))

        def kept(rows):
            out((rows, lanes), pl.BlockSpec((rows, lanes), lambda i: (0, 0)))

        n_x = 2 * p + (p if ahead else 0)
        if product:
            if split:
                for _ in range(q):
                    kept(2 * p)
            else:
                out((2 * q * p, lanes), pl.BlockSpec((2 * p, lanes), lambda i: (jnp.minimum(i, q - 1), 0)))
            kept(2 * p)
            for _ in range(1, q):
                kept(n_x)
        n_made = len(out_shape)
        if near:
            out((4 * q * p // 2, lanes))
        n_results = len(results)
        if results:
            factor, before = into
            in_specs.append(pl.BlockSpec(factor.shape, lambda i: (0, 0, 0)))
            args.append(factor)
            for x in before:
                aliases[len(args)] = len(out_shape) + len(aliases)
                in_specs.append(HBM)
                args.append(x)
            out(self.v.shape)
            out(self.v.shape)
            nbytes += 8 * q * p * lanes * n_results
        in_specs += [HBM] * len(after)
        args += list(after)
        n_in = len(args)

        def kernel(*refs):
            data, rest = refs[:n_data], list(refs[n_data:n_in])
            outs = refs[n_in : n_in + len(out_shape)]
            arrived, scaled, staged, sems = refs[n_in + len(out_shape) :]
            inner = data[0][1] == 1
            r, per = data[0][0], data[0][4]
            i = pl.program_id(0)
            if product:
                w_ref, near_ref, far_ref = rest[:3]
                z_refs, own_ref = outs[: n_made - q], outs[n_made - q]
                x_refs = outs[n_made - q + 1 : n_made]
                rest = rest[3:]
            near_out = outs[n_made] if near else None

            def near_copies():
                return self.copies(data, near, staged, sems, 0)

            def line_copies():
                return self.copies(data, lines, staged, sems, 0)

            def relay_copies():
                return [c for k, b in enumerate(relay) for c in self.copies(data, [b], x_refs[k], sems, 2 * q + k)]

            def ahead_copies():
                return [
                    pltpu.make_async_copy(b[0](data), x_refs[k].at[pl.ds(2 * p, p), :], sems.at[3 * q + k])
                    for k, b in enumerate(ahead)
                ]

            def result_copies(side):
                return [
                    c
                    for j, blocks in enumerate(results)
                    for k, b in enumerate(blocks[side])
                    for c in self.copies(data, [b], arrived.at[j * q + k], sems, 7 * q + 1 + (3 * j) * q + k)
                ]

            def near_copy():
                return pltpu.make_async_copy(staged, near_out, sems.at[7 * q])

            def slab_of(j, k):
                return lax.rem(r - k + q, q) * per + results[j][0][0]

            def leaving():
                return [
                    pltpu.make_async_copy(
                        scaled.at[j * q + k, pl.ds(f * p, p), :],
                        outs[-2 + f].at[slab_of(j, k), :, pl.ds(results[j][0][1], lanes)],
                        sems.at[7 * q + 1 + (3 * j + 1) * q + 2 * k + f],
                    )
                    for j in range(n_results)
                    for k in range(q)
                    for f in range(2)
                ]

            def start(copies):
                for c in copies:
                    c.start()

            def wait(copies):
                for c in copies:
                    c.wait()

            @pl.when(i == 0)
            def _():
                start(ahead_copies())

                @pl.when(inner)
                def _():
                    start(result_copies(1))
                    start(near_copies())

                @pl.when(jnp.logical_not(inner))
                def _():
                    start(line_copies())
                    start(result_copies(2))
                    start(relay_copies())

            if product:
                half = near_ref.shape[0]
                acc = jnp.dot(w_ref[:, :half], near_ref[...], preferred_element_type=F32)
                acc += jnp.dot(w_ref[:, half:], far_ref[...], preferred_element_type=F32)
                acc = acc.astype(BF)
                for k in range(q):
                    z_ref = z_refs[k] if split else z_refs[0]

                    @pl.when((i == k) & (inner | (not lines)))
                    def _():
                        z_ref[...] = acc

                    if lines and 2 * k * p < q * p:

                        @pl.when((i == k) & jnp.logical_not(inner))
                        def _():
                            if k == 0:
                                wait(line_copies())
                            z_ref[...] = staged[2 * k * p : 2 * (k + 1) * p]

                @pl.when(i == q)
                def _():
                    own_ref[...] = acc

                for k in range(1, q):

                    @pl.when((i == q + k) & (inner | (not relay)))
                    def _():
                        x_refs[k - 1][pl.ds(0, 2 * p), :] = acc

            @pl.when(i == min(1, steps - 1))
            def _():
                if near:

                    @pl.when(inner)
                    def _():
                        wait(near_copies())
                        near_copy().start()

                if results:
                    wait(result_copies(1))
                    for j in range(n_results):
                        for k in range(q):
                            f = rest[0][lax.rem(slab_of(j, k), self.kx), :, pl.ds(results[j][0][1], lanes)]
                            scaled[j * q + k] = (arrived[j * q + k].astype(F32) * f).astype(BF)
                    start(leaving())

            @pl.when(i == steps - 1)
            def _():
                wait(ahead_copies())

                @pl.when(inner)
                def _():
                    if near:
                        near_copy().wait()

                @pl.when(jnp.logical_not(inner))
                def _():
                    wait(relay_copies())

                wait(leaving())

        made = pl.pallas_call(
            kernel,
            grid=(steps,),
            in_specs=in_specs,
            out_specs=out_specs,
            out_shape=out_shape,
            scratch_shapes=[
                pltpu.VMEM((max(n_results, 1) * q, 2 * p, lanes), BF),
                pltpu.VMEM((max(n_results, 1) * q, 2 * p, lanes), BF),
                pltpu.VMEM((2 * q * p, lanes), BF),
                pltpu.SemaphoreType.DMA((7 * q + 1 + 3 * n_results * q,)),
            ],
            input_output_aliases=aliases,
            compiler_params=params(),
            cost_estimate=cost(4 * flops, 4 * nbytes),
            name="step",
        )(*args)
        made = list(made)
        return made[:n_made], made[n_made : n_made + 1] if near else None, made[-2:] if results else None


def rounds(axis, n, first=0, last=0):
    if n & (n - 1):
        return [lambda x: lax.psum(x, axis)]
    steps = sorted((1 << k for k in range(n.bit_length() - 1)), key=lambda step: (step != first, step == last, -step))
    return [lambda x, step=step: x + lax.ppermute(x, axis, [(i, i ^ step) for i in range(n)]) for step in steps]


def local(sizes, kz, velocity, kx_index, kz_index, helm_even, helm_odd, deriv_even, deriv_odd):
    n, n_span = sizes
    c, kx, p, cols = velocity.shape
    q = n // 4
    slabs = c * kx
    per = slabs // q
    lanes = cols // 2
    v = velocity.reshape(slabs, p, cols)
    me = lax.axis_index("wall")
    quarter, r = me // q, me % q
    high = quarter >= 2
    inner = (quarter == 1) | (quarter == 2)
    place = jnp.stack([r, inner.astype(jnp.int32), high.astype(jnp.int32), jnp.int32(q), jnp.int32(per)]).astype(jnp.int32)

    def pairs(quarters, shift=0):
        return [(a * q + j, b * q + (j + shift) % q) for a, b in quarters for j in range(q)]

    own = [(a, a) for a in range(4)]
    own_inner = [(1, 1), (2, 2)]
    to_inner, to_outer, middle = [(0, 1), (3, 2)], [(1, 0), (2, 3)], [(1, 2), (2, 1)]

    def send(x, quarters, shift=0):
        return lax.ppermute(x, "wall", pairs(quarters, shift))

    chunks = [(t, lane) for t in range(per) for lane in (0, lanes)]
    total = len(chunks)
    sizes = (q, p, lanes, kx)
    n_whole, n_within = min(HOP, per), min(HOP + 1, per)
    mine_cut, within, outer, near, far = {}, {}, {}, {}, {}

    def cut_slabs(shifts, slabs_, after, mib=24):
        return cut(place, v, [(k, t, 1, 0, cols) for t in slabs_ for k in shifts], after, mib)

    def gather(t, cuts, mine=None):
        mine_cut[t] = cuts[0]
        within[t] = [send(x, own, k + 1) for k, x in enumerate(mine or cuts[1:])]
        outer[t] = [send(x, to_inner, k) for k, x in enumerate(cuts)]

    def within_block(step, i, k):
        t, lane = chunks[i]
        if t < n_within:
            return step.block(within[t][k - 1], 0, p, lane, 0)
        return step.block(x_sent[i - 3 * HOP][k - 1], 2 * p, p)

    def own_lines(step, i):
        t, lane = chunks[i]
        first = step.block(mine_cut[t], 0, p, lane, 0) if t < n_whole else step.planes(0, chunks[i])
        return [first] + [within_block(step, i, k) for k in range(1, q)]

    def near_blocks(step, i):
        t, lane = chunks[i]
        if t < n_whole:
            return own_lines(step, i) + [step.block(x, 0, p, lane, 0) for x in outer[t]]
        return own_lines(step, i) + [step.block(z_sent[i - 2 * HOP], 0, q * p)]

    def make_near(i, after):
        step = Step(sizes, place, v)
        _, (near[i],), _ = step.call(near=near_blocks(step, i), after=after)
        far[i] = send(near[i], middle)

    wall_rounds = rounds("wall", n, n // 2, n // 4)
    spare = [(k, t, 1, 0, cols) for t in range(n_whole, n_within) for k in range(1, q)]
    cuts = list(cut(place, v, [(k, 0, 1, 0, cols) for k in range(q)] + spare, (), 56))
    cuts, spare = cuts[:q], cuts[q:]
    energy = wall_rounds[0](energy_of(v))
    gather(0, pass_on(cuts, [energy]), cuts[1:])
    w = operators(helm_even, helm_odd, deriv_even, deriv_odd, place, high, r, q, ())
    x_sent, z_sent, own_out = {}, {}, {}
    for t in range(n_whole, n_within):
        within[t] = [send(x, own, k + 1) for k, x in enumerate(spare[: q - 1])]
    make_near(0, [w] + (within[n_whole] if n_whole < n_within else []))
    for add in wall_rounds[1:]:
        energy = add(energy)
    for t in range(1, n_whole):
        gather(t, cut_slabs(range(q), [t], [near[0], energy]))
    make_near(1, [])

    def factor_of(energy):
        scale = jnp.float32(float(c * kx * n * p * cols * n_span)) / energy[0, 0]
        kx_sq = (kx_index.astype(F32) / XMODES) ** 2
        kz_sq = (kz_index.astype(F32) / kz) ** 2
        return scale * (1.0 / (1.0 + 2.0 * (kx_sq[:, None, None] + kz_sq[None, None, :])))

    factor = None
    out = []
    for i in range(total + LAG):
        step = Step(sizes, place, v)
        options = {}
        if i < total:
            options["product"] = (w, near[i], far[i])
            options["split"] = i >= total - 2 * HOP
            if i == 0:
                options["after"] = [energy]
            if i == 1:
                energy, _ = lax.optimization_barrier((energy, own_out[0]))
                for add in rounds("span", n_span):
                    energy = add(energy)
                factor = factor_of(energy)
            if 0 < i and i + HOP < total:
                options["near"] = near_blocks(step, i + HOP)
            if i + 2 * HOP < total:
                options["lines"] = own_lines(step, i + 2 * HOP)
            if i + 3 * HOP < total:
                options["ahead"] = [step.planes(k, chunks[i + 3 * HOP]) for k in range(1, q)]
            if HOP <= i < total - HOP:
                options["relay"] = [step.block(z_sent[i - HOP], 2 * k * p, 2 * p) for k in range(1, q)]
        done = [d for d, lag in ((i - LAG, LAG), (i - HOP, HOP)) if 0 <= d < total and (d >= total - 2 * HOP) == (lag == HOP)]
        if i >= total and not done:
            continue
        options["results"] = []
        for d in done:
            mine = [step.block(own_out[d], 0, 2 * p)] + [step.block(x, 0, 2 * p) for x in x_sent[d]]
            if d < total - 2 * HOP:
                theirs = [step.block(z_sent[d], 0, 2 * p)] + [step.block(x, 0, 2 * p) for x in x_sent[d + HOP]]
            else:
                theirs = [step.block(x, 0, 2 * p) for x in z_sent[d]]
            options["results"].append((chunks[d], mine, theirs))
        if done:
            options["into"] = (factor, out)
        made, later, out_new = step.call(**options)
        out = out_new or out
        if i < total:
            if later:
                (near[i + HOP],) = later
                far[i + HOP] = send(near[i + HOP], middle)
            if options["split"]:
                z_sent[i] = [send(x, to_outer, k) for k, x in enumerate(made[:q])]
            else:
                z_sent[i] = send(made[0], to_outer + to_inner if "lines" in options else to_outer)
            own_out[i] = made[-q]
            x_sent[i] = [send(x, own, k + 1) for k, x in enumerate(made[len(made) - q + 1 :])]
            if i == 0 and HOP < total:
                make_near(HOP, made[-q : len(made) - q + 1])
    updated, shear = out
    return updated.reshape(velocity.shape), shear.reshape(velocity.shape)


def solution(mesh):
    sizes = (mesh.shape["wall"], mesh.shape["span"])

    def whole(velocity, *rest):
        body = functools.partial(local, sizes, velocity.shape[3])
        in_specs = (P(None, None, "wall", "span"), P(), P("span"), P(), P(), P(), P())
        out_specs = (P(None, None, "wall", "span"), P(None, None, "wall", "span"))
        return jax.shard_map(body, mesh=mesh, in_specs=in_specs, out_specs=out_specs, check_vma=False)(velocity, *rest)

    return whole
```

```python
import functools

import jax
import jax.numpy as jnp
from jax import lax
from jax.experimental import pallas as pl
from jax.experimental.pallas import tpu as pltpu
from jax.sharding import PartitionSpec as P

BF = jnp.bfloat16
F32 = jnp.float32
XMODES = 5120
HOP = 2
LAG = 2 * HOP
HBM = pl.BlockSpec(memory_space=pltpu.HBM)
SMEM = pl.BlockSpec(memory_space=pltpu.SMEM)
VMEM = pl.BlockSpec(memory_space=pltpu.VMEM)


def params(mib=24):
    return pltpu.CompilerParams(vmem_limit_bytes=mib * 1024 * 1024)


def cost(flops, nbytes):
    return pl.CostEstimate(flops=int(flops), bytes_accessed=int(nbytes), transcendentals=0)


def operator_kernel(block, place_ref, rows_ref, cols_ref, *refs):
    given, (w_ref, held, source, sems) = refs[:4], refs[-4:]
    h = rows_ref.shape[0]
    p = block
    copies = [pltpu.make_async_copy(x, held.at[i], sems.at[i]) for i, x in enumerate(given)]
    for copy in copies:
        copy.start()
    half = jnp.where(place_ref[2] == 1, -0.5, 0.5).astype(F32)
    from_row = lax.broadcasted_iota(jnp.int32, (h, h), 1)
    pick_rows = jnp.where(from_row == rows_ref[...], 1.0, 0.0).astype(BF)

    def product(a, b):
        return jnp.dot(a, b, preferred_element_type=F32)

    def combine(field, even, odd, factor):
        source[0, field] = product(pick_rows, ((even + odd) * factor).astype(BF)).astype(BF)
        source[1, field] = product(pick_rows, ((even - odd) * factor).astype(BF)).astype(BF)

    copies[0].wait()
    copies[1].wait()
    combine(0, held[0].astype(F32), held[1].astype(F32), 0.5)
    copies[2].wait()
    copies[3].wait()
    combine(1, product(held[2], held[0]), product(held[3], held[1]), half)
    for side in range(2):
        from_col = lax.broadcasted_iota(jnp.int32, (h, h), 0)
        pick_cols = jnp.where(from_col == cols_ref[side : side + 1, :], 1.0, 0.0).astype(BF)
        for field in range(2):
            picked = product(source[side, field], pick_cols)
            for s in range(h // p):
                at = (2 * s + field) * p
                w_ref[at : at + p, side * h : (side + 1) * h] = picked[s * p : (s + 1) * p].astype(BF)


def operators(helm_even, helm_odd, deriv_even, deriv_odd, place, high, r, q, after):
    h = helm_even.shape[0]
    p = h // (2 * q)
    low = jnp.logical_not(high)

    def order(part, member, plane, flipped):
        index = (part * q + member) * p + plane
        return jnp.where(flipped, h - 1 - index, index)

    index = lax.iota(jnp.int32, h)
    part, step, plane = index // (q * p), index // p % q, index % p
    to, came = (r + step) % q, (r - step + q) % q
    rows = order(jnp.where(low, part, 1 - part), to, plane, high)
    near = order(jnp.where(low, 1 - part, part), came, plane, high)
    far = order(jnp.where(low, part, 1 - part), came, plane, low)
    return pl.pallas_call(
        functools.partial(operator_kernel, p),
        in_specs=[SMEM, VMEM, VMEM] + [HBM] * (4 + len(after)),
        out_specs=VMEM,
        out_shape=jax.ShapeDtypeStruct((2 * h, 2 * h), BF),
        scratch_shapes=[pltpu.VMEM((4, h, h), BF), pltpu.VMEM((2, 2, h, h), BF), pltpu.SemaphoreType.DMA((4,))],
        compiler_params=params() if p % 16 == 0 else params(48),
        cost_estimate=cost(20 * h**3, 16 * h * h),
        name="operators",
    )(place, rows[:, None], jnp.stack([near, far]), helm_even, helm_odd, deriv_even, deriv_odd, *after)


def energy_kernel(v_ref, *refs):
    out_ref, total = refs[-2:]
    i = pl.program_id(0)
    wide = v_ref[...].astype(F32)
    part = jnp.sum((wide * wide).reshape(-1, *total.shape), axis=0)

    @pl.when(i == 0)
    def _():
        total[...] = part

    @pl.when(i > 0)
    def _():
        total[...] += part

    @pl.when(i == pl.num_programs(0) - 1)
    def _():
        out_ref[...] = jnp.sum(jnp.sum(total[...], axis=0, keepdims=True), axis=1, keepdims=True)


def energy_of(v, after):
    slabs, p, cols = v.shape
    block = 2 if slabs % 2 == 0 else 1
    return pl.pallas_call(
        energy_kernel,
        grid=(slabs // block,),
        in_specs=[pl.BlockSpec((block * p, cols), lambda i: (i, 0))] + [HBM] * len(after),
        out_specs=pl.BlockSpec((1, 1), lambda i: (0, 0)),
        out_shape=jax.ShapeDtypeStruct((1, 1), F32),
        scratch_shapes=[pltpu.VMEM((8, cols), F32)],
        compiler_params=params(),
        cost_estimate=cost(0, 2 * v.size),
        name="energy",
    )(v.reshape(slabs * p, cols), *after)


def cut_kernel(pieces, place_ref, v_ref, *refs):
    outs, stages, (sems,) = refs[-2 * len(pieces) - 1 : -len(pieces) - 1], refs[-len(pieces) - 1 : -1], refs[-1:]
    q, per = place_ref[3], place_ref[4]
    read, write = [], []
    for i, (shift, t0, count, lane, width) in enumerate(pieces):
        first = lax.rem(place_ref[0] + shift, q) * per + t0
        source = v_ref.at[pl.ds(first, count), :, pl.ds(lane, width)]
        read.append(pltpu.make_async_copy(source, stages[i], sems.at[0, i]))
        write.append(pltpu.make_async_copy(stages[i], outs[i], sems.at[1, i]))
    for copy in read:
        copy.start()
    for i in range(len(pieces)):
        read[i].wait()
        write[i].start()
    for copy in write:
        copy.wait()


def cut(place, v, pieces, after, mib=24):
    p = v.shape[1]
    shapes = [(count, p, width) for _, _, count, _, width in pieces]
    return pl.pallas_call(
        functools.partial(cut_kernel, pieces),
        in_specs=[SMEM, HBM] + [HBM] * len(after),
        out_specs=[HBM] * len(pieces),
        out_shape=[jax.ShapeDtypeStruct(shape, BF) for shape in shapes],
        scratch_shapes=[pltpu.VMEM(shape, BF) for shape in shapes] + [pltpu.SemaphoreType.DMA((2, len(pieces)))],
        compiler_params=params(mib),
        cost_estimate=cost(0, 4 * p * sum(count * width for _, _, count, _, width in pieces)),
        name="cut",
    )(place, v, *after)


def pass_on_kernel(n, *refs):
    given, made, stages, (sems,) = refs[:n], refs[-2 * n - 1 : -n - 1], refs[-n - 1 : -1], refs[-1:]
    read = [pltpu.make_async_copy(given[i], stages[i], sems.at[0, i]) for i in range(n)]
    write = [pltpu.make_async_copy(stages[i], made[i], sems.at[1, i]) for i in range(n)]
    for copy in read:
        copy.start()
    for i in range(n):
        read[i].wait()
        write[i].start()
    for copy in write:
        copy.wait()


def pass_on(arrays, after):
    n = len(arrays)
    return pl.pallas_call(
        functools.partial(pass_on_kernel, n),
        in_specs=[HBM] * (n + len(after)),
        out_specs=[HBM] * n,
        out_shape=[jax.ShapeDtypeStruct(x.shape, BF) for x in arrays],
        scratch_shapes=[pltpu.VMEM(x.shape, BF) for x in arrays] + [pltpu.SemaphoreType.DMA((2, n))],
        compiler_params=params(56),
        cost_estimate=cost(0, 4 * sum(x.size for x in arrays)),
        name="pass_on",
    )(*arrays, *after)


class Step:
    def __init__(self, sizes, place, v):
        self.q, self.p, self.lanes, self.kx = sizes
        self.place, self.v = place, v
        self.operands = [place, v]
        self.sems = 0

    def block(self, array, row, count, lane=0, lead=None):
        known = [i for i, x in enumerate(self.operands) if x is array]
        if not known:
            self.operands.append(array)
        k = known[0] if known else len(self.operands) - 1

        def ref(refs):
            rows, cols = pl.ds(row, count), pl.ds(lane, self.lanes)
            return refs[k].at[rows, cols] if lead is None else refs[k].at[lead, rows, cols]

        return ref, count

    def planes(self, shift, chunk):
        slab, lane = chunk

        def ref(refs):
            first = lax.rem(refs[0][0] + shift, self.q) * refs[0][4] + slab
            return refs[1].at[first, :, pl.ds(lane, self.lanes)]

        return ref, self.p

    def copies(self, refs, blocks, target, sems, first):
        made, row = [], 0
        for i, (ref, count) in enumerate(blocks):
            made.append(pltpu.make_async_copy(ref(refs), target.at[pl.ds(row, count), :], sems.at[first + i]))
            row += count
        return made

    def call(self, product=None, near=(), lines=(), relay=(), ahead=(), results=(), into=None, split=False, after=()):
        q, p, lanes = self.q, self.p, self.lanes
        n_data = len(self.operands)
        steps = 2 * q if product else 1
        in_specs = [SMEM] + [HBM] * (n_data - 1)
        args = list(self.operands)
        flops = nbytes = 0
        if product:
            w = product[0]
            depth = w.shape[1]
            in_specs += [pl.BlockSpec((2 * p, depth), lambda i: (i, 0))]
            in_specs += [pl.BlockSpec(product[1].shape, lambda i: (0, 0))] * 2
            args += list(product)
            flops += 2 * depth * depth * lanes
            nbytes += 2 * depth * (depth + 2 * lanes)
        out_specs, out_shape, aliases = [], [], {}

        def out(shape, spec=HBM):
            out_specs.append(spec)
            out_shape.append(jax.ShapeDtypeStruct(shape, BF))

        def kept(rows):
            out((rows, lanes), pl.BlockSpec((rows, lanes), lambda i: (0, 0)))

        n_x = 2 * p + (p if ahead else 0)
        if product:
            if split:
                for _ in range(q):
                    kept(2 * p)
            else:
                out((2 * q * p, lanes), pl.BlockSpec((2 * p, lanes), lambda i: (jnp.minimum(i, q - 1), 0)))
            kept(2 * p)
            for _ in range(1, q):
                kept(n_x)
        n_made = len(out_shape)
        if near:
            out((4 * q * p // 2, lanes))
        n_results = len(results)
        if results:
            factor, before = into
            in_specs.append(pl.BlockSpec(factor.shape, lambda i: (0, 0, 0)))
            args.append(factor)
            for x in before:
                aliases[len(args)] = len(out_shape) + len(aliases)
                in_specs.append(HBM)
                args.append(x)
            out(self.v.shape)
            out(self.v.shape)
            nbytes += 8 * q * p * lanes * n_results
        in_specs += [HBM] * len(after)
        args += list(after)
        n_in = len(args)

        def kernel(*refs):
            data, rest = refs[:n_data], list(refs[n_data:n_in])
            outs = refs[n_in : n_in + len(out_shape)]
            arrived, scaled, staged, sems = refs[n_in + len(out_shape) :]
            inner = data[0][1] == 1
            r, per = data[0][0], data[0][4]
            i = pl.program_id(0)
            if product:
                w_ref, near_ref, far_ref = rest[:3]
                z_refs, own_ref = outs[: n_made - q], outs[n_made - q]
                x_refs = outs[n_made - q + 1 : n_made]
                rest = rest[3:]
            near_out = outs[n_made] if near else None

            def near_copies():
                return self.copies(data, near, staged, sems, 0)

            def line_copies():
                return self.copies(data, lines, staged, sems, 0)

            def relay_copies():
                return [c for k, b in enumerate(relay) for c in self.copies(data, [b], x_refs[k], sems, 2 * q + k)]

            def ahead_copies():
                return [
                    pltpu.make_async_copy(b[0](data), x_refs[k].at[pl.ds(2 * p, p), :], sems.at[3 * q + k])
                    for k, b in enumerate(ahead)
                ]

            def result_copies(side):
                return [
                    c
                    for j, blocks in enumerate(results)
                    for k, b in enumerate(blocks[side])
                    for c in self.copies(data, [b], arrived.at[j * q + k], sems, 7 * q + 1 + (3 * j) * q + k)
                ]

            def near_copy():
                return pltpu.make_async_copy(staged, near_out, sems.at[7 * q])

            def slab_of(j, k):
                return lax.rem(r - k + q, q) * per + results[j][0][0]

            def leaving():
                return [
                    pltpu.make_async_copy(
                        scaled.at[j * q + k, pl.ds(f * p, p), :],
                        outs[-2 + f].at[slab_of(j, k), :, pl.ds(results[j][0][1], lanes)],
                        sems.at[7 * q + 1 + (3 * j + 1) * q + 2 * k + f],
                    )
                    for j in range(n_results)
                    for k in range(q)
                    for f in range(2)
                ]

            def start(copies):
                for c in copies:
                    c.start()

            def wait(copies):
                for c in copies:
                    c.wait()

            @pl.when(i == 0)
            def _():
                start(ahead_copies())

                @pl.when(inner)
                def _():
                    start(result_copies(1))
                    start(near_copies())

                @pl.when(jnp.logical_not(inner))
                def _():
                    start(line_copies())
                    start(result_copies(2))
                    start(relay_copies())

            if product:
                half = near_ref.shape[0]
                acc = jnp.dot(w_ref[:, :half], near_ref[...], preferred_element_type=F32)
                acc += jnp.dot(w_ref[:, half:], far_ref[...], preferred_element_type=F32)
                acc = acc.astype(BF)
                for k in range(q):
                    z_ref = z_refs[k] if split else z_refs[0]

                    @pl.when((i == k) & (inner | (not lines)))
                    def _():
                        z_ref[...] = acc

                    if lines and 2 * k * p < q * p:

                        @pl.when((i == k) & jnp.logical_not(inner))
                        def _():
                            if k == 0:
                                wait(line_copies())
                            z_ref[...] = staged[2 * k * p : 2 * (k + 1) * p]

                @pl.when(i == q)
                def _():
                    own_ref[...] = acc

                for k in range(1, q):

                    @pl.when((i == q + k) & (inner | (not relay)))
                    def _():
                        x_refs[k - 1][pl.ds(0, 2 * p), :] = acc

            @pl.when(i == min(1, steps - 1))
            def _():
                if near:

                    @pl.when(inner)
                    def _():
                        wait(near_copies())
                        near_copy().start()

                if results:
                    wait(result_copies(1))
                    for j in range(n_results):
                        for k in range(q):
                            f = rest[0][lax.rem(slab_of(j, k), self.kx), :, pl.ds(results[j][0][1], lanes)]
                            scaled[j * q + k] = (arrived[j * q + k].astype(F32) * f).astype(BF)
                    start(leaving())

            @pl.when(i == steps - 1)
            def _():
                wait(ahead_copies())

                @pl.when(inner)
                def _():
                    if near:
                        near_copy().wait()

                @pl.when(jnp.logical_not(inner))
                def _():
                    wait(relay_copies())

                wait(leaving())

        made = pl.pallas_call(
            kernel,
            grid=(steps,),
            in_specs=in_specs,
            out_specs=out_specs,
            out_shape=out_shape,
            scratch_shapes=[
                pltpu.VMEM((max(n_results, 1) * q, 2 * p, lanes), BF),
                pltpu.VMEM((max(n_results, 1) * q, 2 * p, lanes), BF),
                pltpu.VMEM((2 * q * p, lanes), BF),
                pltpu.SemaphoreType.DMA((7 * q + 1 + 3 * n_results * q,)),
            ],
            input_output_aliases=aliases,
            compiler_params=params(),
            cost_estimate=cost(4 * flops, 4 * nbytes),
            name="step",
        )(*args)
        made = list(made)
        return made[:n_made], made[n_made : n_made + 1] if near else None, made[-2:] if results else None


def rounds(axis, n, first=0, last=0):
    if n & (n - 1):
        return [lambda x: lax.psum(x, axis)]
    steps = sorted((1 << k for k in range(n.bit_length() - 1)), key=lambda step: (step != first, step == last, -step))
    return [lambda x, step=step: x + lax.ppermute(x, axis, [(i, i ^ step) for i in range(n)]) for step in steps]


def local(sizes, kz, velocity, kx_index, kz_index, helm_even, helm_odd, deriv_even, deriv_odd):
    n, n_span = sizes
    c, kx, p, cols = velocity.shape
    q = n // 4
    slabs = c * kx
    per = slabs // q
    lanes = cols // 2
    v = velocity.reshape(slabs, p, cols)
    me = lax.axis_index("wall")
    quarter, r = me // q, me % q
    high = quarter >= 2
    inner = (quarter == 1) | (quarter == 2)
    place = jnp.stack([r, inner.astype(jnp.int32), high.astype(jnp.int32), jnp.int32(q), jnp.int32(per)]).astype(jnp.int32)

    def pairs(quarters, shift=0):
        return [(a * q + j, b * q + (j + shift) % q) for a, b in quarters for j in range(q)]

    own = [(a, a) for a in range(4)]
    own_inner = [(1, 1), (2, 2)]
    to_inner, to_outer, middle = [(0, 1), (3, 2)], [(1, 0), (2, 3)], [(1, 2), (2, 1)]

    def send(x, quarters, shift=0):
        return lax.ppermute(x, "wall", pairs(quarters, shift))

    chunks = [(t, lane) for t in range(per) for lane in (0, lanes)]
    total = len(chunks)
    sizes = (q, p, lanes, kx)
    n_whole, n_within = min(HOP, per), min(HOP + 1, per)
    mine_cut, within, outer, near, far = {}, {}, {}, {}, {}

    def cut_slabs(shifts, slabs_, after, mib=24):
        return cut(place, v, [(k, t, 1, 0, cols) for t in slabs_ for k in shifts], after, mib)

    def gather(t, cuts, mine=None):
        mine_cut[t] = cuts[0]
        within[t] = [send(x, own, k + 1) for k, x in enumerate(mine or cuts[1:])]
        outer[t] = [send(x, to_inner, k) for k, x in enumerate(cuts)]

    def within_block(step, i, k):
        t, lane = chunks[i]
        if t < n_within:
            return step.block(within[t][k - 1], 0, p, lane, 0)
        return step.block(x_sent[i - 3 * HOP][k - 1], 2 * p, p)

    def own_lines(step, i):
        t, lane = chunks[i]
        first = step.block(mine_cut[t], 0, p, lane, 0) if t < n_whole else step.planes(0, chunks[i])
        return [first] + [within_block(step, i, k) for k in range(1, q)]

    def near_blocks(step, i):
        t, lane = chunks[i]
        if t < n_whole:
            return own_lines(step, i) + [step.block(x, 0, p, lane, 0) for x in outer[t]]
        return own_lines(step, i) + [step.block(z_sent[i - 2 * HOP], 0, q * p)]

    def make_near(i, after):
        step = Step(sizes, place, v)
        _, (near[i],), _ = step.call(near=near_blocks(step, i), after=after)
        far[i] = send(near[i], middle)

    wall_rounds = rounds("wall", n, n // 2, n // 4)
    spare = [(k, t, 1, 0, cols) for t in range(n_whole, n_within) for k in range(1, q)]
    cuts = list(cut(place, v, [(k, 0, 1, 0, cols) for k in range(q)] + spare, (), 56))
    cuts, spare = cuts[:q], cuts[q:]
    energy = wall_rounds[0](energy_of(v, cuts[:1]))
    gather(0, pass_on(cuts, [energy]), cuts[1:])
    w = operators(helm_even, helm_odd, deriv_even, deriv_odd, place, high, r, q, ())
    x_sent, z_sent, own_out = {}, {}, {}
    for t in range(n_whole, n_within):
        within[t] = [send(x, own, k + 1) for k, x in enumerate(spare[: q - 1])]
    make_near(0, [w] + (within[n_whole] if n_whole < n_within else []))
    for add in wall_rounds[1:]:
        energy = add(energy)
    for t in range(1, n_whole):
        gather(t, cut_slabs(range(q), [t], [near[0], energy]))
    make_near(1, [])

    def factor_of(energy):
        scale = jnp.float32(float(c * kx * n * p * cols * n_span)) / energy[0, 0]
        kx_sq = (kx_index.astype(F32) / XMODES) ** 2
        kz_sq = (kz_index.astype(F32) / kz) ** 2
        return scale * (1.0 / (1.0 + 2.0 * (kx_sq[:, None, None] + kz_sq[None, None, :])))

    factor = None
    out = []
    for i in range(total + LAG):
        step = Step(sizes, place, v)
        options = {}
        if i < total:
            options["product"] = (w, near[i], far[i])
            options["split"] = i >= total - 2 * HOP
            if i == 0:
                options["after"] = [energy]
            if i == 1:
                energy, _ = lax.optimization_barrier((energy, own_out[0]))
                for add in rounds("span", n_span):
                    energy = add(energy)
                factor = factor_of(energy)
            if 0 < i and i + HOP < total:
                options["near"] = near_blocks(step, i + HOP)
            if i + 2 * HOP < total:
                options["lines"] = own_lines(step, i + 2 * HOP)
            if i + 3 * HOP < total:
                options["ahead"] = [step.planes(k, chunks[i + 3 * HOP]) for k in range(1, q)]
            if HOP <= i < total - HOP:
                options["relay"] = [step.block(z_sent[i - HOP], 2 * k * p, 2 * p) for k in range(1, q)]
        done = [d for d, lag in ((i - LAG, LAG), (i - HOP, HOP)) if 0 <= d < total and (d >= total - 2 * HOP) == (lag == HOP)]
        if i >= total and not done:
            continue
        options["results"] = []
        for d in done:
            mine = [step.block(own_out[d], 0, 2 * p)] + [step.block(x, 0, 2 * p) for x in x_sent[d]]
            if d < total - 2 * HOP:
                theirs = [step.block(z_sent[d], 0, 2 * p)] + [step.block(x, 0, 2 * p) for x in x_sent[d + HOP]]
            else:
                theirs = [step.block(x, 0, 2 * p) for x in z_sent[d]]
            options["results"].append((chunks[d], mine, theirs))
        if done:
            options["into"] = (factor, out)
        made, later, out_new = step.call(**options)
        out = out_new or out
        if i < total:
            if later:
                (near[i + HOP],) = later
                far[i + HOP] = send(near[i + HOP], middle)
            if options["split"]:
                z_sent[i] = [send(x, to_outer, k) for k, x in enumerate(made[:q])]
            else:
                z_sent[i] = send(made[0], to_outer + to_inner if "lines" in options else to_outer)
            own_out[i] = made[-q]
            x_sent[i] = [send(x, own, k + 1) for k, x in enumerate(made[len(made) - q + 1 :])]
            if i == 0 and HOP < total:
                make_near(HOP, made[-q : len(made) - q + 1])
    updated, shear = out
    return updated.reshape(velocity.shape), shear.reshape(velocity.shape)


def solution(mesh):
    sizes = (mesh.shape["wall"], mesh.shape["span"])

    def whole(velocity, *rest):
        body = functools.partial(local, sizes, velocity.shape[3])
        in_specs = (P(None, None, "wall", "span"), P(), P("span"), P(), P(), P(), P())
        out_specs = (P(None, None, "wall", "span"), P(None, None, "wall", "span"))
        return jax.shard_map(body, mesh=mesh, in_specs=in_specs, out_specs=out_specs, check_vma=False)(velocity, *rest)

    return whole
```
